32 devices in a mesh: dp: 16 (over z, y, x), tensor: 2 (over core).
Axes of the slice: x: 2, y: 2, z: 4, core: 2. Of those that a mesh axis runs over, the one named last changes fastest.
Arguments:
- inputs: bfloat16 [32768, 512], P(('dp', 'tensor')), may hold values from -6 to 6
- lengths: int32 [128], P('dp'), may hold values from 1 to 250, 12288 in all
- w_query: bfloat16 [512, 512], P(None, 'tensor'), may hold values from -0.25 to 0.25
- w_key: bfloat16 [512, 512], P(None, 'tensor'), may hold values from -0.25 to 0.25
- w_value: bfloat16 [512, 512], P(None, 'tensor'), may hold values from -0.25 to 0.25
- w_attn_out: bfloat16 [512, 512], P('tensor'), may hold values from -1.25 to 1.25
- gain_attn: float32 [512], replicated, may hold values from 0.5 to 1.5
- offset_attn: float32 [512], replicated, may hold values from -2 to 2
- w_in: bfloat16 [512, 2048], P(None, 'tensor'), may hold values from -0.25 to 0.25
- b_in: bfloat16 [2048], P('tensor'), may hold values from -3 to 3
- w_out: bfloat16 [2048, 512], P('tensor'), may hold values from -0.125 to 0.125
- b_out: float32 [512], replicated, may hold values from -2 to 2
- gain_ffn: float32 [512], replicated, may hold values from 0.5 to 1.5
- offset_ffn: float32 [512], replicated, may hold values from -2 to 2
- cotangent: bfloat16 [32768, 512], P(('dp', 'tensor')), may hold values from -6 to 6
Outputs:
- output: bfloat16 [32768, 512], P(('dp', 'tensor'))
- grad_inputs: float32 [32768, 512], P(('dp', 'tensor'))
- grad_query: float32 [512, 512], P(None, 'tensor')
- grad_key: float32 [512, 512], P(None, 'tensor')
- grad_value: float32 [512, 512], P(None, 'tensor')
- grad_attn_out: float32 [512, 512], P('tensor')
- grad_gain_attn: float32 [512], replicated
- grad_offset_attn: float32 [512], replicated
- grad_w_in: float32 [512, 2048], P(None, 'tensor')
- grad_b_in: float32 [2048], P('tensor')
- grad_w_out: float32 [2048, 512], P('tensor')
- grad_b_out: float32 [512], replicated
- grad_gain_ffn: float32 [512], replicated
- grad_offset_ffn: float32 [512], replicated
The draws below stay inside these ranges and needn't reach their ends.
Inputs may be any that keep to these rules, and one draw needn't show every extreme that they name: Batch row b holds one sentence of lengths[b] subwords at its first positions; the rest of its 256 positions are padding.
All inputs are finite; a program needn't handle non-finite values. No bound on the sum of `lengths` on one device may be relied on, other than what follows from the above.
Results may differ from the reference program's by a relative error of at most 0.039.
Values may be sent and summed in bfloat16 or wider, within the bound.
A program may use at most 192 MiB of HBM per device.

```python
import math
import jax
import jax.numpy as jnp
import numpy as np
from jax import lax

D = 512
HEADS = 8
FF = 2048
HEAD_DIM = 64
SEQ = 256
RECUR = 2
BATCH = 128
TOKENS = 32768


def level_of(own_key, extent, pieces, least, top_value):
    loudness = 1.0
    for position, parts in pieces:
        steps = jax.random.uniform(jax.random.fold_in(jax.random.fold_in(own_key, 6), position), (parts,), jnp.float32, least / len(pieces), top_value / len(pieces))
        loudness = loudness * jnp.repeat(jnp.exp(steps), extent[position] // parts).reshape((-1,) + (1,) * (len(extent) - 1 - position))
    return loudness


def length_profile(amount, total, most, slope):
    portions = [(1 << 20) // math.isqrt(standing ** slope) + 1 for standing in range(2, amount + 1)]
    spare, given = total - most - (amount - 1), [1] * (amount - 1)
    while spare > 0:
        movable = [i for i in range(amount - 1) if given[i] < most]
        whole, remaining = sum([portions[i] for i in movable]), spare
        for i in movable:
            more = min(most - given[i], max(1, remaining * portions[i] // whole), spare)
            given[i] = given[i] + more
            spare = spare - more
    return np.array([most] + given)


def uneven(own_key, number_of, total, reach, skew):
    if number_of == 2:
        one = jax.random.randint(own_key, (), max(1, total - reach), min(reach, total - 1) + 1)
        return jnp.stack([one, total - one])
    sizes = jnp.asarray(length_profile(number_of, total, reach, skew), jnp.int32)
    twos = (number_of - 1) // 2
    donor, receiver = sizes[1:1 + 2 * twos:2], sizes[2:2 + 2 * twos:2]
    slack = jnp.minimum(donor - 1, reach - receiver)
    moved = jax.random.randint(jax.random.fold_in(own_key, 1), (twos,), 0, 1 << 20) % (slack + 1)
    sizes = sizes.at[1:1 + 2 * twos:2].set(donor - moved).at[2:2 + 2 * twos:2].set(receiver + moved)
    return sizes[jax.random.permutation(jax.random.fold_in(own_key, 2), number_of)]


def gaussian(stream_key, shape, deviation, reach, split=(), dtype=jnp.bfloat16):
    drawn = deviation * jax.random.normal(stream_key, shape, jnp.float32)
    if split:
        drawn = drawn * level_of(stream_key, shape, split, -0.22, 0.18)
    return jnp.clip(drawn, -reach, reach).astype(dtype)


def setup_inputs(seed: int = 0) -> dict:
    splits = jax.random.split(jax.random.key(seed), 16)
    inputs = gaussian(splits[0], (TOKENS, D), 1.0, 6.0, ((0, 32),))
    lengths = uneven(splits[1], BATCH, BATCH * min(96, SEQ // 2), min(250, SEQ), 2).astype(jnp.int32)
    w_query = gaussian(splits[2], (D, D), D ** -0.5, 0.25, ((1, 2),))
    w_key = gaussian(splits[3], (D, D), D ** -0.5, 0.25, ((1, 2),))
    w_value = gaussian(splits[4], (D, D), D ** -0.5, 0.25, ((1, 2),))
    w_attn_out = gaussian(splits[5], (D, D), 24 ** -0.5, 1.25, ((0, 2),))
    gain_attn = jnp.clip(1.0 + 0.1 * jax.random.normal(splits[6], (D,), jnp.float32), 0.5, 1.5)
    offset_attn = gaussian(splits[7], (D,), 0.3, 2.0, (), jnp.float32)
    w_in = gaussian(splits[8], (D, FF), D ** -0.5, 0.25, ((1, 2),))
    b_in = gaussian(splits[9], (FF,), 0.5, 3.0, ((0, 2),))
    w_out = gaussian(splits[10], (FF, D), FF ** -0.5, 0.125, ((0, 2),))
    b_out = gaussian(splits[11], (D,), 0.3, 2.0, (), jnp.float32)
    gain_ffn = jnp.clip(1.0 + 0.1 * jax.random.normal(splits[12], (D,), jnp.float32), 0.5, 1.5)
    offset_ffn = gaussian(splits[13], (D,), 0.3, 2.0, (), jnp.float32)
    cotangent = gaussian(splits[14], (TOKENS, D), 1.0, 6.0, ((0, 32),))
    return {"inputs": inputs, "lengths": lengths, "w_query": w_query, "w_key": w_key, "w_value": w_value, "w_attn_out": w_attn_out, "gain_attn": gain_attn, "offset_attn": offset_attn, "w_in": w_in, "b_in": b_in, "w_out": w_out, "b_out": b_out, "gain_ffn": gain_ffn, "offset_ffn": offset_ffn, "cotangent": cotangent}


@jax.custom_vjp
def low(v):
    return lax.optimization_barrier(v.astype(jnp.bfloat16)).astype(jnp.float32)

@jax.custom_vjp
def low_back(v):
    return v

def low_keep(v):
    return (low(v), None)

def low_pass(kept, grad):
    return (grad,)

def back_keep(v):
    return (v, None)

def back_low(kept, grad):
    return (low(grad),)
low.defvjp(low_keep, low_pass)
low_back.defvjp(back_keep, back_low)
epsilon = 1e-05
masked_score = -1e+30
highest = lax.Precision.HIGHEST

def layer_norm(resid, gain_vec, offset):
    row_mean = lax.optimization_barrier(jnp.mean(resid, axis=-1, keepdims=True))
    centred = resid - row_mean
    spread = lax.optimization_barrier(jnp.mean(centred * centred, axis=-1, keepdims=True))
    return centred * lax.rsqrt(spread + epsilon) * gain_vec + offset

def layer(stream, sent_lens, params):
    w_query, w_key, w_value, w_attn_out, gain_attn, offset_attn, w_in, b_in, w_out, b_out, gain_ffn, offset_ffn = params
    group_rows = stream.shape[0]
    rows_low = low(stream)

    def project(weight):
        product = jnp.einsum('gsd,de->gse', rows_low, weight, precision=highest)
        return low(low_back(product)).reshape(group_rows, SEQ, HEADS, HEAD_DIM)
    queries = project(w_query)
    key_block = project(w_key)
    values = project(w_value)
    scores = low_back(jnp.einsum('gqhd,gkhd->ghqk', queries, key_block, precision=highest) * HEAD_DIM ** (-0.5))
    places = lax.broadcasted_iota(jnp.int32, (group_rows, SEQ), 1)
    usable = places < sent_lens[:, None]
    scores = jnp.where(usable[:, None, None, :], scores, masked_score)
    probability = low(jax.nn.softmax(scores, axis=-1))
    context = low(low_back(jnp.einsum('ghqk,gkhd->gqhd', probability, values, precision=highest)))
    context = context.reshape(group_rows, SEQ, D)
    branch_attn = low_back(jnp.einsum('gsc,cd->gsd', context, w_attn_out, precision=highest))
    middle = layer_norm(stream + branch_attn, gain_attn, offset_attn)
    hidden = low_back(jnp.einsum('gsd,df->gsf', low(middle), w_in, precision=highest) + b_in)
    active = low(jax.nn.gelu(hidden))
    branch_ffn = low_back(jnp.einsum('gsf,fd->gsd', active, w_out, precision=highest) + b_out)
    return layer_norm(middle + branch_ffn, gain_ffn, offset_ffn)

def reference(inputs, lengths, w_query, w_key, w_value, w_attn_out, gain_attn, offset_attn, w_in, b_in, w_out, b_out, gain_ffn, offset_ffn, cotangent):
    group_size = math.gcd(BATCH, 16)
    params = tuple((weight.astype(jnp.float32) for weight in (w_query, w_key, w_value, w_attn_out, gain_attn, offset_attn, w_in, b_in, w_out, b_out, gain_ffn, offset_ffn)))
    stream = inputs.astype(jnp.float32).reshape(BATCH // group_size, group_size, SEQ, D)
    sent_lens = lengths.reshape(BATCH // group_size, group_size)

    def run(stream_all, weights):

        def block(record):
            result = record[0]
            for recurrence in range(RECUR):
                result = layer(result, record[1], weights)
            return result
        return lax.map(jax.checkpoint(block), (stream_all, sent_lens))
    result, back = jax.vjp(run, stream, params)
    grad_stream, grad_params = back(cotangent.astype(jnp.float32).reshape(result.shape))
    return (result.reshape(TOKENS, D).astype(jnp.bfloat16), grad_stream.reshape(TOKENS, D), grad_params[0], grad_params[1], grad_params[2], grad_params[3], grad_params[4], grad_params[5], grad_params[6], grad_params[7], grad_params[8], grad_params[9], grad_params[10], grad_params[11])
```

```python
import functools

import jax
import jax.numpy as jnp
from jax import lax
from jax.experimental import pallas as pl
from jax.experimental.pallas import tpu as pltpu
from jax.sharding import PartitionSpec as P

HEAD_DIM = 64
SEQ = 256
PAIR = 2 * HEAD_DIM
CHUNK = 512
BLOCK = 256
LEAST = 16
GROUP = 2
FORWARD_TURNS = (12, 1, 3, 1, 1, 8, 1, 1, 1, 3, 1, 1, 1, 2, 1, 1, 1, 1, 1, 2, 1, 3)
BACKWARD_TURNS = (8, 1, 1, 1, 1, 1, 1, 1, 1, 1, 1, 1, 1, 1, 1, 1)
LAST_TURNS = (3, 1, 1, 1, 1, 1, 1, 1, 1, 1, 1, 3)
ROWS = 32
EPS = 1e-05
MASKED = -1e30
SCALE = HEAD_DIM ** (-0.5)
GELU_A = 0.7978845608028654
GELU_B = GELU_A * 0.044715
BF16 = jnp.bfloat16
F32 = jnp.float32
MIB = 1 << 20
STEPS_AT = (
    (),
    (),
    ((0, 1),),
    ((1, 1),),
    ((0, 2), (2, 1)),
    ((1, 2),),
    ((0, 3),),
    ((1, 3), (3, 1)),
    (),
    ((4, 1),),
    ((3, 2),),
    ((2, 2), (5, 1)),
    ((0, 4),),
    ((1, 4), (4, 2)),
    ((3, 3), (0, 5)),
    ((2, 3),),
    ((1, 5),),
    ((3, 4), (5, 2)),
    ((4, 3),),
    ((0, 6), (3, 5)),
    ((2, 4), (6, 1), (1, 6)),
    ((4, 4), (5, 3), (7, 1), (8, 1)),
    ((2, 5), (0, 7), (3, 6)),
)
STEPS_LEFT = (
    (6, 2), (1, 7), (4, 5), (5, 4), (7, 2), (8, 2), (2, 6), (3, 7),
    (6, 3), (4, 6), (5, 5), (7, 3), (8, 3), (6, 4), (2, 7), (7, 4),
    (8, 4), (4, 7), (5, 6), (6, 5), (7, 5), (2, 8), (8, 5), (5, 7),
    (6, 6), (7, 6), (8, 6), (6, 7), (2, 9), (7, 7), (8, 7),
)
SMALL_AT = (7, 9, 12, 15, 18)
Z_FIRST = (2,)


def mm(a, b):
    return lax.dot_general(a, b, (((1,), (0,)), ((), ())), preferred_element_type=F32)


def mm_rt(a, b):
    return lax.dot_general(a, b, (((1,), (1,)), ((), ())), preferred_element_type=F32)


def mm_lt(a, b):
    return lax.dot_general(a, b, (((0,), (0,)), ((), ())), preferred_element_type=F32)


def low(v):
    return v.astype(BF16)


def norm(v):
    centred = v - jnp.mean(v, axis=-1, keepdims=True)
    root = lax.rsqrt(jnp.mean(centred * centred, axis=-1, keepdims=True) + EPS)
    return centred * root, root


def norm_back(d, n, root, gain):
    dn = d * gain
    first = jnp.mean(dn, axis=-1, keepdims=True)
    second = jnp.mean(dn * n, axis=-1, keepdims=True)
    return (dn - first - n * second) * root


def fold(v):
    return jnp.sum(v.reshape(v.shape[0] // 8, 8, v.shape[1]), axis=0)


def halves_by_rows(out, fn, n_sums, *arrays):
    joined, sums = [], None
    rows = arrays[0].shape[0]
    for r in range(0, rows, ROWS):
        got = fn(*(a[r : r + ROWS] for a in arrays))
        cut = len(got) - n_sums
        joined.append(got[:cut])
        sums = got[cut:] if sums is None else [a + b for a, b in zip(sums, got[cut:])]
        if r + ROWS == rows // 2:
            yield
    out += [jnp.concatenate(parts, axis=0) for parts in zip(*joined)]
    out += [jnp.sum(s, axis=0, keepdims=True) for s in sums]


def by_rows(fn, n_sums, *arrays):
    out = []
    for _ in halves_by_rows(out, fn, n_sums, *arrays):
        pass
    return out


def head_masks(dtype, value):
    lane = lax.broadcasted_iota(jnp.int32, (1, PAIR), 1)
    first = jnp.where(lane < HEAD_DIM, value, 0.0).astype(dtype)
    second = jnp.where(lane < HEAD_DIM, 0.0, value).astype(dtype)
    return first, second


def lanes(start, size):
    return pl.ds(pl.multiple_of(start, PAIR), size)


def interleave(first, second, turns):
    for i, turn in enumerate(turns):
        for _ in range(turn):
            next((first, second)[i % 2], None)
    for stream in (first, second):
        for _ in stream:
            pass


def attend(qkv, rows, probs, slab, d, key_bias, contexts):
    masks = head_masks(BF16, SCALE)
    heads = d // HEAD_DIM
    qs, ks, v_ts = [], [], []
    for col in range(0, d, PAIR):
        qs.append(qkv[rows, col : col + PAIR])
        ks.append(qkv[rows, d + col : d + col + PAIR])
        v_ts.append(qkv[rows, 2 * d + col : 2 * d + col + PAIR].T)
    scores, ps, halves = {}, {}, []
    for n in range(heads + 2):
        if n < heads:
            scores[n] = mm_rt(ks[n // 2], qs[n // 2] * masks[n % 2])
        if 1 <= n <= heads:
            full = scores.pop(n - 1)
            sides = []
            for c in range(0, SEQ, PAIR):
                s = full[:, c : c + PAIR] + key_bias
                e = jnp.exp(s - jnp.max(s, axis=0, keepdims=True))
                sides.append(low(e * (1.0 / jnp.sum(e, axis=0, keepdims=True))))
            ps[n - 1] = jnp.concatenate(sides, axis=1)
            probs[slab + n - 1] = ps[n - 1]
        if n >= 2:
            h = (n - 2) % 2
            halves.append(
                mm(v_ts[(n - 2) // 2][h * HEAD_DIM : (h + 1) * HEAD_DIM], ps.pop(n - 2))
            )
        yield
    contexts += [
        low(jnp.concatenate(halves[2 * i : 2 * i + 2], axis=0)) for i in range(heads // 2)
    ]


def attend_back(qkv, rows, probs, slab, d, grad_ctx, start, heads):
    masks, ones = head_masks(BF16, SCALE), head_masks(BF16, 1.0)
    qs, ks, vs, k_ts, gs = [], [], [], [], []
    for col in range(start * HEAD_DIM, (start + heads) * HEAD_DIM, PAIR):
        qs.append(qkv[rows, col : col + PAIR])
        ks.append(qkv[rows, d + col : d + col + PAIR])
        vs.append(qkv[rows, 2 * d + col : 2 * d + col + PAIR])
        k_ts.append(ks[-1].T)
        gs.append(grad_ctx[:, col - start * HEAD_DIM : col - start * HEAD_DIM + PAIR])
    d_p, g_hs, ps, d_s, d_q, out = {}, {}, {}, {}, {}, []
    for n in range(heads + 2):
        if n < heads:
            g_hs[n] = gs[n // 2] * ones[n % 2]
            ps[n] = probs[slab + start + n]
            d_p[n] = mm_rt(vs[n // 2], g_hs[n])
        if 1 <= n <= heads:
            full, p = d_p.pop(n - 1), ps[n - 1]
            sides = []
            for c in range(0, SEQ, PAIR):
                wide = p[:, c : c + PAIR].astype(F32)
                prod = full[:, c : c + PAIR] * wide
                sides.append(low(prod - wide * jnp.sum(prod, axis=0, keepdims=True)))
            d_s[n - 1] = jnp.concatenate(sides, axis=1)
        if n >= 2:
            m = n - 2
            pair, h = m // 2, m % 2
            d_q[m] = mm(k_ts[pair][h * HEAD_DIM : (h + 1) * HEAD_DIM], d_s[m])
            if h == 1:
                both = (m - 1, m)
                d_v = mm(
                    jnp.concatenate([ps[i] for i in both], axis=1),
                    jnp.concatenate([g_hs[i] for i in both], axis=0),
                )
                d_k = mm(
                    jnp.concatenate([d_s[i] for i in both], axis=1),
                    jnp.concatenate([qs[pair] * masks[i % 2] for i in both], axis=0),
                )
                q_t = low(jnp.concatenate([d_q[i] for i in both], axis=0) * SCALE)
                out.append((q_t.T, low(d_k), low(d_v)))
        yield
    for pair, grads in enumerate(out):
        for i, grad in enumerate(grads):
            col = i * d + start * HEAD_DIM + pair * PAIR
            qkv[rows, col : col + PAIR] = grad


def axis_sizes(n_dp):
    k = round((n_dp / 2) ** (1 / 3))
    return (k, k, 2 * k) if 2 * k**3 == n_dp else (1, 1, n_dp)


def unit_blocks(half_ff):
    n = half_ff // BLOCK
    tall_pairs = [(b, b + 1) for b in range(2, n, 2)]
    wide_pairs = [(b, b + 1) for b in range(n + 1, 2 * n + 1, 2)]
    return [(0,), (1,)] + tall_pairs + [(n,)] + wide_pairs + [(2 * n + i,) for i in range(1, 4)]


def unit_sizes(d, half_ff):
    return [d * len(blocks) for blocks in unit_blocks(half_ff)]


def unit_orders(count):
    return [(2, 3) if u in Z_FIRST else (0, 1) for u in range(count)]


def stage_plan(sizes, order, rows, coords):
    x, y, z = (((a, 1, sizes[a]),) for a in range(3))
    z_bits = tuple((2, 1 << b, 2) for b in range(sizes[2].bit_length() - 1))
    first, second = (y, x) if order % 2 else (x, y)
    walk = first + second + z if order < 2 else z_bits[:1] + first + second + z_bits[1:]
    off, plan = 0, []
    for axis, step, n in walk:
        if n == 1:
            continue
        at = coords[axis]
        place = (at // step) % n
        split = rows % (LEAST * n) == 0
        rows = rows // n if split else rows
        moves = []
        for k in range(1, n):
            to, back = (place + k) % n, (place + n - k) % n
            moves.append((
                at + (to - place) * step,
                off + to * rows if split else off,
                off + back * rows if split else off,
            ))
        off = off + place * rows if split else off
        plan.append((axis, split, rows, off, moves))
    return plan


def land_rows(sizes, units):
    orders = unit_orders(len(units))
    return sum(
        stage[2] * len(stage[4])
        for rows, halves in zip(units, orders)
        for order in halves
        for stage in stage_plan(sizes, order, rows // 2, (0, 0, 0))
    )


def layers_kernel(
    t_rows, sizes, lens, x_hbm, cot_hbm, wq_hbm, wk_hbm, wv_hbm, wo_hbm, w1_hbm, w2_hbm, b1_own,
    gain_a_ref, off_a_ref, bias_o_ref, gain_f_ref, off_f_ref,
    out_ref, gx_ref, gq_ref, gk_ref, gv_ref, go_ref, g1_ref, g2_ref, small_out,
    wqkv, w_o, w_1, w_2, b_1, b_half, x_buf, stream,
    qkv, probs, x_t, ctx_t, mid_t, act_n, gp, n_1, n_2, roots, g_ffn, g_attn,
    gb1_sum, theirs, whole, landing, small_v, small_r,
    in_sem, w_sem, w_send, w_recv, out_sem, put_sem, pair_send, pair_recv, send_sem, sum_recv,
    all_recv, done_sem, small_send, small_recv,
):
    d = w_o.shape[0]
    ff = w_1.shape[1]
    heads = d // HEAD_DIM
    group = x_buf.shape[0]
    per_group = group // SEQ
    n_groups = t_rows // group
    half_d, half_ff = d // 2, ff // 2
    side, dp = lax.axis_index("tensor"), lax.axis_index("dp")
    other = 1 - side
    gain_a, off_a, bias_o, gain_f, off_f = (
        r[...] for r in (gain_a_ref, off_a_ref, bias_o_ref, gain_f_ref, off_f_ref)
    )
    first = side * (t_rows // SEQ)
    strides = (1, sizes[0], sizes[0] * sizes[1])
    coords = tuple((dp // strides[a]) % sizes[a] for a in range(3))
    units = unit_sizes(d, half_ff)
    n_ffn = half_ff // BLOCK
    in_unit = unit_blocks(half_ff)
    n_blocks = 2 * n_ffn + 4
    unit_of = [u for u, blocks in enumerate(in_unit) for _ in blocks]
    tall = units[-1]

    def along(axis, to):
        return dp + (to - coords[axis]) * strides[axis]

    peers = [(dp, other)]
    for a in range(3):
        peers += [(along(a, (coords[a] + k) % sizes[a]), side) for k in range(1, sizes[a])]
    barrier = pltpu.get_barrier_semaphore()
    for peer in peers:
        pl.semaphore_signal(barrier, inc=1, device_id=peer, device_id_type=pl.DeviceIdType.MESH)
    pl.semaphore_wait(barrier, len(peers))

    def remote(src, dst, send, recv, dp_to, side_to):
        return pltpu.make_async_remote_copy(
            src_ref=src, dst_ref=dst, send_sem=send, recv_sem=recv,
            device_id=(dp_to, side_to), device_id_type=pl.DeviceIdType.MESH,
        )

    def span(i, n):
        return pl.ds(pl.multiple_of(i * n, n), n)

    def own_cols(base):
        return pl.ds(pl.multiple_of(base + side * half_d, half_d), half_d)

    weights = [
        (wq_hbm, wqkv.at[:, own_cols(0)]),
        (wk_hbm, wqkv.at[:, own_cols(d)]),
        (wv_hbm, wqkv.at[:, own_cols(2 * d)]),
        (wo_hbm, w_o.at[span(side, half_d), :]),
        (w1_hbm, w_1.at[:, span(side, half_ff)]),
        (w2_hbm, w_2.at[span(side, half_ff), :]),
    ]
    b_half[side] = b1_own[...].astype(F32)
    bias_copy = remote(
        b_half.at[side], b_half.at[side], w_send.at[6], w_recv.at[6], dp, other
    )
    for i, (src, dst) in enumerate(weights):
        if i == 5:
            bias_copy.start()
        remote(src, dst, w_send.at[i], w_recv.at[i], dp, other).start()
        pltpu.make_async_copy(src, dst, w_sem.at[i]).start()

    def have(now, indices):
        @pl.when(now == 0)
        def _():
            for i in indices:
                src, dst = weights[i]
                pltpu.make_async_copy(src, dst, w_sem.at[i]).wait()
                remote(src, dst, w_send.at[i], w_recv.at[i], dp, other).wait()
            if len(weights) - 1 in indices:
                bias_copy.wait()
                count, width = b_half.shape[1:]
                for n in range(2 * count):
                    b_1[:, n * width : (n + 1) * width] = b_half[n // count, n % count : n % count + 1, :]

    gb1_sum[...] = jnp.zeros_like(gb1_sum)
    small_v[0] = jnp.zeros_like(small_v[0])

    def at(layer, g):
        return pl.ds(pl.multiple_of(layer * t_rows + g * group, group), group)

    def at_sentence(layer, s):
        return pl.ds(pl.multiple_of(layer * t_rows + s * SEQ, SEQ), SEQ)

    def fetch_x(g):
        return pltpu.make_async_copy(x_hbm.at[at(0, g), :], x_buf, in_sem.at[0])

    def fetch_cot(g):
        return pltpu.make_async_copy(cot_hbm.at[at(0, g), :], x_buf, in_sem.at[1])

    fetch_x(0).start()

    kept = (t_rows // SEQ) * heads

    def slab_of(layer, s, in_group):
        return jnp.where(layer == 0, s, t_rows // SEQ + in_group) * heads

    n_chunks = ff // CHUNK

    def chunk(c):
        return slice(c * CHUNK, (c + 1) * CHUNK)

    def forward(g, layer, i):
        s = g * per_group + i
        rows, local = at_sentence(layer, s), slice(i * SEQ, (i + 1) * SEQ)
        x_low = low(stream[local, :])
        x_t[:, rows] = x_low.T
        for c in range(3 * d // CHUNK):
            qkv[rows, chunk(c)] = low(mm(x_low, wqkv[:, chunk(c)]))
            yield
        place = lax.broadcasted_iota(jnp.int32, (SEQ, PAIR), 0)
        key_bias = jnp.where(place < lens[first + s], 0.0, MASKED)
        contexts = []
        yield from attend(qkv, rows, probs, slab_of(layer, s, i), d, key_bias, contexts)
        for j, context in enumerate(contexts):
            ctx_t[j * PAIR : (j + 1) * PAIR, rows] = context
        context = jnp.concatenate([context.T for context in contexts], axis=1)
        if i == 0:
            have(g + layer, range(3, len(weights)))
        branch = mm(context, w_o[...])
        yield

        def first_norm(x, branch):
            n, root = norm(x + branch)
            middle = n * gain_a + off_a
            return low(n), root, middle + bias_o, low(middle)

        out = []
        yield from halves_by_rows(out, first_norm, 0, stream[local, :], branch)
        n, root, total, mid_low = out
        n_1[layer, local, :] = n
        roots[layer, local, 0:1] = root
        mid_t[:, rows] = mid_low.T
        yield
        hidden, acts = {}, {}
        for c in range(n_chunks + 2):
            if c < n_chunks:
                hidden[c] = mm(mid_low, w_1[:, chunk(c)])
            if 1 <= c <= n_chunks:
                last = chunk(c - 1)

                def activate(h):
                    h = low(h + b_1[:, last])
                    sq = h * h
                    t = jnp.tanh(h * (sq * GELU_B + GELU_A))
                    half_up = t * 0.5 + 0.5
                    act = h * half_up
                    return act, half_up + act * (1.0 - t) * (sq * (3.0 * GELU_B) + GELU_A)

                acts[c - 1], slope = by_rows(activate, 0, hidden.pop(c - 1))
                gp[rows, last] = slope
                act_n[rows, last] = acts[c - 1]
            if c >= 2:
                total = total + mm(acts.pop(c - 2), w_2[chunk(c - 2), :])
            yield

        def second_norm(v):
            n, root = norm(v)
            return low(n), root, n * gain_f + off_f

        out = []
        yield from halves_by_rows(out, second_norm, 0, total)
        n, root, result = out
        n_2[layer, local, :] = n
        roots[layer, local, 1:2] = root
        stream[local, :] = result
        yield

    def backward_norm(layer, g, i):
        rows, local = at_sentence(layer, g * per_group + i), slice(i * SEQ, (i + 1) * SEQ)

        def second_norm(grad, n, root):
            n = n.astype(F32)
            g_sum = norm_back(grad, n, root, gain_f)
            return g_sum, low(g_sum), fold(grad * n), fold(grad), fold(g_sum)

        out = []
        yield from halves_by_rows(
            out, second_norm, 3, stream[local, :], n_2[layer, local, :], roots[layer, local, 1:2]
        )
        g_mid, g_low, *sums = out
        for j, total in zip((2, 3, 4), sums):
            small_v[0, j : j + 1, :] += total
        g_ffn[rows, :] = g_low
        stream[local, :] = g_mid
        yield

    def backward_ffn(layer, g, i):
        rows, local = at_sentence(layer, g * per_group + i), slice(i * SEQ, (i + 1) * SEQ)
        g_mid, g_low = stream[local, :], g_ffn[rows, :]
        g_act, g_hid = {}, {}
        for c in range(n_chunks + 2):
            if c < n_chunks:
                g_act[c] = mm_rt(g_low, w_2[chunk(c), :])
            if 1 <= c <= n_chunks:
                last = chunk(c - 1)

                def through(g, slope):
                    g_h = g * slope.astype(F32)
                    return low(g_h), fold(g_h)

                g_hid[c - 1], total = by_rows(through, 1, g_act.pop(c - 1), gp[rows, last])
                gb1_sum[:, last] += total
                gp[rows, last] = g_hid[c - 1]
            if c >= 2:
                g_mid = g_mid + mm_rt(g_hid.pop(c - 2), w_1[:, chunk(c - 2)])
            yield

        def first_norm(grad, n, root):
            n = n.astype(F32)
            g_res = norm_back(grad, n, root, gain_a)
            return g_res, low(g_res), fold(grad * n), fold(grad)

        out = []
        yield from halves_by_rows(
            out, first_norm, 2, g_mid, n_1[layer, local, :], roots[layer, local, 0:1]
        )
        g_res, g_low, *sums = out
        for j, total in zip((0, 1), sums):
            small_v[0, j : j + 1, :] += total
        g_attn[rows, :] = g_low
        if layer == 1:
            stream[local, :] = g_res
        yield

    def backward_attn(layer, g, i, part, parts):
        s = g * per_group + i
        rows, some = at_sentence(layer, s), heads // parts
        at_part = slice(part * some * HEAD_DIM, (part + 1) * some * HEAD_DIM)
        grad_ctx = low(mm_rt(g_attn[rows, :], w_o[at_part, :]))
        yield
        yield from attend_back(
            qkv, rows, probs, slab_of(layer, s, i), d, grad_ctx, part * some, some
        )

    def backward(g, i):
        local = slice(i * SEQ, (i + 1) * SEQ)
        yield from backward_norm(1, g, i)
        yield from backward_ffn(1, g, i)
        yield from backward_attn(1, g, i, 0, 1)
        rows = at_sentence(1, g * per_group + i)
        total = stream[local, :]
        for c in range(3):
            at_third = slice(c * d, (c + 1) * d)
            total = total + mm_rt(qkv[rows, at_third], wqkv[:, at_third])
            if c == 2:
                stream[local, :] = total
            yield
        yield from backward_norm(0, g, i)

    def both(steps_of, turns):
        if per_group == 2:
            interleave(steps_of(0), steps_of(1), turns)
        else:
            for _ in steps_of(0):
                pass

    starts = [sum(units[:u]) for u in range(len(units))]
    plans, landed = [], 0
    for rows, orders in zip(units, unit_orders(len(units))):
        halves = []
        for order in orders:
            plan = []
            for axis, split, n, own, moves in stage_plan(sizes, order, rows // 2, coords):
                plan.append((axis, split, n, own, moves, landed))
                landed += n * len(moves)
            halves.append(plan)
        plans.append(halves)
    stages = [max(len(plan) for plan in halves) for halves in plans]

    def unit_rows(u, half, start, n):
        return pl.ds(pl.multiple_of(starts[u] + half * (units[u] // 2) + start, LEAST), n)

    def acc_at(start, n):
        return probs.at[kept + start // BLOCK, pl.ds(pl.multiple_of(start % BLOCK, LEAST), n), :]

    def half_row(u, half, start):
        return starts[u] + half * (units[u] // 2) + start

    def pair_copy(b):
        return remote(
            theirs.at[b % 2], whole.at[b * tall : (b + 1) * tall, :],
            pair_send.at[b], pair_recv.at[unit_of[b]], dp, other,
        )

    def send_sums(u, half, i):
        axis, _, n, _, moves, land = plans[u][half][i]
        for k, (to, give, _) in enumerate(moves):
            remote(
                acc_at(half_row(u, half, give), n), landing.at[land + k * n : land + (k + 1) * n, :],
                send_sem.at[u], sum_recv.at[u, half, i], along(axis, to), side,
            ).start()

    def send_all(u, half, i):
        while i >= 0 and not plans[u][half][i][1]:
            i -= 1
        if i < 0:
            return
        axis, _, n, own, moves, _ = plans[u][half][i]
        for to, _, _ in moves:
            rows = unit_rows(u, half, own, n)
            remote(
                whole.at[rows, :], whole.at[rows, :], send_sem.at[u], all_recv.at[u, half, i],
                along(axis, to), side,
            ).start()

    def arrived(rows, sem):
        pltpu.make_async_copy(whole.at[0:rows, :], whole.at[0:rows, :], sem).wait()

    def sent_rows(u):
        return sum(
            n * len(moves) * (2 if split else 1)
            for plan in plans[u]
            for _, split, n, _, moves, _ in plan
        )

    def done_copies(u):
        copies = []
        for b in in_unit[u]:
            if b > n_ffn:
                first_col = (b - n_ffn - 1) * BLOCK
                out = (
                    g1_ref.at[:, first_col : first_col + BLOCK] if b <= 2 * n_ffn
                    else (gq_ref, gk_ref, gv_ref)[b - 2 * n_ffn - 1]
                )
                copies.append(pltpu.make_async_copy(
                    whole.at[b * tall : (b + 1) * tall, :], out, done_sem.at[b, 0]
                ))
                continue
            for c in range(2):
                row = b * tall + c * BLOCK
                cols = slice(c * BLOCK, (c + 1) * BLOCK)
                rows = slice(b * BLOCK, (b + 1) * BLOCK)
                out = g2_ref.at[rows, cols] if b < n_ffn else go_ref.at[:, cols]
                copies.append(pltpu.make_async_copy(
                    whole.at[row : row + BLOCK, :], out, done_sem.at[b, c]
                ))
        return copies

    def step_pair(u):
        arrived(units[u], pair_recv.at[u])

        def add(i, carry):
            rows = pl.ds(pl.multiple_of(starts[u] + i * BLOCK, BLOCK), BLOCK)
            at_slab = kept + starts[u] // BLOCK + i
            probs[at_slab] = probs[at_slab] + whole[rows, :]
            return carry

        lax.fori_loop(0, units[u] // BLOCK, add, 0)
        for half in range(2):
            send_sums(u, half, 0)

    def step_sum(i, u):
        for half in range(2):
            if i >= len(plans[u][half]):
                continue
            _, _, n, own, moves, land = plans[u][half][i]
            arrived(n * len(moves), sum_recv.at[u, half, i])
            mine = acc_at(half_row(u, half, own), n)
            total = mine[...]
            for k in range(len(moves)):
                total = total + landing[land + k * n : land + (k + 1) * n, :]
            if i + 1 < len(plans[u][half]):
                mine[...] = total
                send_sums(u, half, i + 1)
            else:
                whole[unit_rows(u, half, own, n), :] = total
                send_all(u, half, i)

    def step_all(i, u):
        for half in range(2):
            if i < len(plans[u][half]) and plans[u][half][i][1]:
                _, _, n, _, moves, _ = plans[u][half][i]
                arrived(n * len(moves), all_recv.at[u, half, i])
                send_all(u, half, i - 1)
        if i == 0:
            for copy in done_copies(u):
                copy.start()

    def run_step(u, step):
        if step == 1:
            step_pair(u)
        elif step <= 1 + stages[u]:
            step_sum(step - 2, u)
        else:
            step_all(2 * stages[u] + 1 - step, u)

    small_peers = [(dp, other)]
    bits = (sizes[0] * sizes[1] * sizes[2]).bit_length() - 1
    for bit in range(bits):
        small_peers.append((dp + (1 << bit) * (1 - 2 * ((dp // (1 << bit)) % 2)), side))

    def small_copy(i):
        return remote(
            small_v.at[i], small_r.at[i], small_send.at[i], small_recv.at[i], *small_peers[i]
        )

    def run_small(i):
        small_copy(i).wait()
        small_v[i + 1] = small_v[i] + small_r[i]
        if i + 1 < len(small_peers):
            small_copy(i + 1).start()

    def plain_schedule():
        at_block = list(range(n_ffn)) + [n_ffn + 1 + i for i in range(n_ffn + 1)]
        at_block += [len(STEPS_AT) - 5 + i for i in range(3)]
        born = [at_block[blocks[-1]] for blocks in in_unit]
        count = max(born[u] + 2 * stages[u] + 1 for u in range(len(units))) + 1
        at = [
            [(u, now - born[u]) for u in range(len(units)) if 1 <= now - born[u] <= 2 * stages[u] + 1]
            for now in range(count)
        ]
        return at[: len(STEPS_AT)], [step for now in at[len(STEPS_AT) :] for step in now]

    usual = sizes == (2, 2, 4) and len(units) == 9
    steps_at, steps_left = (STEPS_AT, STEPS_LEFT) if usual else plain_schedule()

    def tick(now):
        if now in SMALL_AT and SMALL_AT.index(now) < len(small_peers):
            run_small(SMALL_AT.index(now))
        for u, step in steps_at[now]:
            run_step(u, step)

    def ticks(i, count, base, stride=1):
        for k in range(count):
            @pl.when(i == k)
            def _():
                tick(base + stride * k)

    def launch(b, value_of):
        def cut(value):
            if value.shape[1] == BLOCK:
                return low(value[:BLOCK]), low(value[BLOCK:])
            return low(value[:, :BLOCK]), low(value[:, BLOCK:])

        for_other, own = cut(value_of(other)), cut(value_of(side))

        @pl.when(b >= 2)
        def _():
            arrived(tall, pair_send.at[b - 2])

        for i in range(2):
            theirs[b % 2, i * BLOCK : (i + 1) * BLOCK, :] = for_other[i]
            probs[kept + 2 * b + i] = own[i]

    def go(i, count, first_block, first_tick):
        for k in range(count):
            @pl.when(i == k)
            def _():
                pair_copy(first_block + k).start()
                tick(first_tick + k)

    def hidden(j, which):
        return pl.ds(pl.multiple_of(which * half_ff + j * BLOCK, BLOCK), BLOCK)

    def out_blocks(j, carry):
        launch(j, lambda which: mm_lt(act_n[:, hidden(j, which)], g_ffn[...]))
        go(j, n_ffn, 0, 0)
        return carry

    def main(g, carry):
        rows = at(0, g)
        fetch_x(g).wait()
        stream[...] = x_buf[...].astype(F32)
        fetch_cot(g).start()
        have(g, range(3))

        def one_layer(layer, inner):
            both(functools.partial(forward, g, layer), FORWARD_TURNS)
            return inner

        lax.fori_loop(0, 2, one_layer, 0)

        put_out = []
        for i in range(group // BLOCK):
            for c in range(d // BLOCK):
                n = per_group * heads + i * (d // BLOCK) + c
                at_cols = slice(c * BLOCK, (c + 1) * BLOCK)
                probs[kept + n] = low(stream[i * BLOCK : (i + 1) * BLOCK, at_cols])
                put_out.append(pltpu.make_async_copy(
                    probs.at[kept + n], out_ref.at[pl.ds(g * group + i * BLOCK, BLOCK), at_cols],
                    put_sem.at[i, c],
                ))
                put_out[-1].start()
        fetch_cot(g).wait()
        stream[...] = x_buf[...].astype(F32)

        @pl.when(g + 1 < n_groups)
        def _():
            fetch_x(g + 1).start()


        both(functools.partial(backward, g), BACKWARD_TURNS)
        for copy in put_out:
            copy.wait()

        @pl.when(g == n_groups - 1)
        def _():
            lax.fori_loop(0, n_ffn, out_blocks, 0)

        both(functools.partial(backward_ffn, 0, g), LAST_TURNS)
        return carry

    lax.fori_loop(0, n_groups, main, 0)
    for c in range(ff // d):
        small_v[0, 8 + c : 9 + c, :] = gb1_sum[:, c * d : (c + 1) * d]

    small_copy(0).start()
    tick(n_ffn)

    launch(n_ffn, lambda which: mm(ctx_t[span(which, half_d), :], g_attn[...]))
    pair_copy(n_ffn).start()
    tick(n_ffn + 1)

    def in_blocks(j, carry):
        launch(n_ffn + 1 + j, lambda which: mm(mid_t[...], gp[:, hidden(j, which)]))
        go(j, n_ffn, n_ffn + 1, n_ffn + 2)
        return carry

    lax.fori_loop(0, n_ffn, in_blocks, 0)
    tick_back = 2 * n_ffn + 2
    tick_q = tick_back + n_groups * per_group * 2

    def back_1(s, carry):
        for part in range(2):
            for _ in backward_attn(0, s // per_group, s % per_group, part, 2):
                pass
            ticks(s, n_groups * per_group, tick_back + part, 2)
        return carry

    lax.fori_loop(0, n_groups * per_group, back_1, 0)

    def qkv_blocks(i, carry):
        launch(
            2 * n_ffn + 1 + i,
            lambda which: mm(x_t[...], qkv[:, lanes(i * d + which * half_d, half_d)]),
        )
        go(i, 3, 2 * n_ffn + 1, tick_q)
        return carry

    lax.fori_loop(0, 3, qkv_blocks, 0)

    def grad_x(g, carry):
        rows = at(0, g)

        @pl.when(g > 0)
        def _():
            pltpu.make_async_copy(x_buf, gx_ref.at[rows, :], out_sem).wait()

        x_buf[...] = low(g_attn[rows, :].astype(F32) + mm_rt(qkv[rows, :], wqkv[...]))
        pltpu.make_async_copy(x_buf, gx_ref.at[rows, :], out_sem).start()
        ticks(g, n_groups, tick_q + 3)
        return carry

    lax.fori_loop(0, n_groups, grad_x, 0)
    for now in range(tick_q + 3 + n_groups, len(steps_at)):
        tick(now)
    for u, step in steps_left:
        run_step(u, step)
    for i in range(len(small_peers)):
        if i >= len(SMALL_AT):
            run_small(i)
    for b in range(n_blocks - 2, n_blocks):
        arrived(tall, pair_send.at[b])
    for u in range(len(units)):
        arrived(sent_rows(u), send_sem.at[u])
    pltpu.make_async_copy(x_buf, gx_ref.at[at(0, 0), :], out_sem).wait()
    small_out[...] = small_v[len(small_peers)]
    for u in range(len(units)):
        for copy in done_copies(u):
            copy.wait()


def layers(n_dp, lens, x, cot, w_q, w_k, w_v, w_o, w_1, w_2, b_1, vectors):
    t_rows, d = x.shape
    half_ff = w_1.shape[1]
    ff = 2 * half_ff
    half_d = d // 2
    heads = d // HEAD_DIM
    sentences = t_rows // SEQ
    group = SEQ * (GROUP if sentences % GROUP == 0 else 1)
    sizes = axis_sizes(n_dp)
    units = unit_sizes(d, half_ff)
    most = 2 + sizes[2].bit_length()
    n_small = n_dp.bit_length()
    vmem = pl.BlockSpec(memory_space=pltpu.VMEM)
    hbm = pl.BlockSpec(memory_space=pl.ANY)
    dma = pltpu.SemaphoreType.DMA
    return pl.pallas_call(
        functools.partial(layers_kernel, t_rows, sizes),
        out_shape=(
            jax.ShapeDtypeStruct((t_rows, d), BF16),
            jax.ShapeDtypeStruct((t_rows, d), BF16),
            jax.ShapeDtypeStruct((d, half_d), BF16),
            jax.ShapeDtypeStruct((d, half_d), BF16),
            jax.ShapeDtypeStruct((d, half_d), BF16),
            jax.ShapeDtypeStruct((half_d, d), BF16),
            jax.ShapeDtypeStruct((d, half_ff), BF16),
            jax.ShapeDtypeStruct((half_ff, d), BF16),
            jax.ShapeDtypeStruct((16, d), F32),
        ),
        in_specs=[pl.BlockSpec(memory_space=pltpu.SMEM)] + [hbm] * 8 + [vmem] * 6,
        out_specs=(hbm,) * 8 + (vmem,),
        scratch_shapes=[
            pltpu.VMEM((d, 3 * d), BF16),
            pltpu.VMEM((d, d), BF16),
            pltpu.VMEM((d, ff), BF16),
            pltpu.VMEM((ff, d), BF16),
            pltpu.VMEM((1, ff), F32),
            pltpu.VMEM((2, 8, half_ff // 8), F32),
            pltpu.VMEM((group, d), BF16),
            pltpu.VMEM((group, d), F32),
            pltpu.VMEM((2 * t_rows, 3 * d), BF16),
            pltpu.VMEM((sentences * heads + max(2 * heads + group // BLOCK * d // BLOCK, sum(units) // BLOCK), SEQ, SEQ), BF16),
            pltpu.VMEM((d, 2 * t_rows), BF16),
            pltpu.VMEM((d, 2 * t_rows), BF16),
            pltpu.VMEM((d, 2 * t_rows), BF16),
            pltpu.VMEM((2 * t_rows, ff), BF16),
            pltpu.VMEM((2 * t_rows, ff), BF16),
            pltpu.VMEM((2, group, d), BF16),
            pltpu.VMEM((2, group, d), BF16),
            pltpu.VMEM((2, group, 2), F32),
            pltpu.VMEM((2 * t_rows, d), BF16),
            pltpu.VMEM((2 * t_rows, d), BF16),
            pltpu.VMEM((1, ff), F32),
            pltpu.VMEM((2, d, BLOCK), BF16),
            pltpu.VMEM((sum(units), BLOCK), BF16),
            pltpu.VMEM((land_rows(sizes, units), BLOCK), BF16),
            pltpu.VMEM((n_small + 1, 16, d), F32),
            pltpu.VMEM((n_small, 16, d), F32),
            dma((2,)),
            dma((7,)),
            dma((7,)),
            dma((7,)),
            dma,
            dma((group // BLOCK, d // BLOCK)),
            dma((sum(units) // d,)),
            dma((len(units),)),
            dma((len(units),)),
            dma((len(units), 2, most)),
            dma((len(units), 2, most)),
            dma((sum(units) // d, 2)),
            dma((n_small,)),
            dma((n_small,)),
        ],
        compiler_params=pltpu.CompilerParams(
            vmem_limit_bytes=63 * MIB, collective_id=0, has_side_effects=True
        ),
        name="layers",
    )(lens, x, cot, w_q, w_k, w_v, w_o, w_1, w_2, b_1, *vectors)


def widen_kernel(per_side, small, *refs):
    count = (len(refs) - 6) // 2
    for src, dst in zip(refs[:count], refs[count : 2 * count]):
        dst[...] = src[...].astype(dst.dtype)
    side = lax.axis_index("tensor")
    for i, ref in enumerate(refs[2 * count : -1]):
        ref[...] = small[i : i + 1, :]
    d = small.shape[1]
    for c in range(per_side):
        first, second = (small[8 + s * per_side + c : 9 + s * per_side + c, :] for s in range(2))
        refs[-1][:, c * d : (c + 1) * d] = jnp.where(side == 0, first, second)


def widen(small, out, wide, half_ff):
    steps = 2
    d = small.shape[1]
    arrays = [out] + wide
    rows = [jax.ShapeDtypeStruct((1, d), F32)] * 5 + [jax.ShapeDtypeStruct((1, half_ff), F32)]

    def cut(a):
        return pl.BlockSpec((a.shape[0] // steps, a.shape[1]), lambda i: (i, 0))

    def fixed(a):
        return pl.BlockSpec(a.shape, lambda i: (0, 0))

    return pl.pallas_call(
        functools.partial(widen_kernel, half_ff // d),
        grid=(steps,),
        out_shape=[jax.ShapeDtypeStruct(out.shape, BF16)]
        + [jax.ShapeDtypeStruct(a.shape, F32) for a in wide]
        + rows,
        in_specs=[fixed(small)] + [cut(a) for a in arrays],
        out_specs=[cut(a) for a in arrays] + [fixed(r) for r in rows],
        compiler_params=pltpu.CompilerParams(vmem_limit_bytes=62 * MIB),
        name="widen",
    )(small, *arrays)


def shards(
    n_dp, inputs, lengths, w_query, w_key, w_value, w_attn_out, gain_attn, offset_attn,
    w_in, b_in, w_out, b_out, gain_ffn, offset_ffn, cotangent,
):
    vectors = [v[None] for v in (gain_attn, offset_attn, b_out, gain_ffn, offset_ffn)]
    out, *wide, small = layers(
        n_dp, lengths, inputs, cotangent, w_query, w_key, w_value, w_attn_out, w_in, w_out,
        b_in.reshape(8, -1), vectors,
    )
    out, gx, g_q, g_k, g_v, g_o, g_1, g_2, s0, s1, s2, s3, s4, gb1 = widen(
        small, out, wide, b_in.shape[0]
    )
    return (
        out, gx, g_q, g_k, g_v, g_o, s0[0], s1[0], g_1, gb1[0], g_2, s4[0], s2[0], s3[0],
    )


def solution(mesh):
    rows = P(("dp", "tensor"), None)
    cols, tall, whole = P(None, "tensor"), P("tensor", None), P()
    in_specs = (
        rows, P("dp"), cols, cols, cols, tall, whole, whole,
        cols, P("tensor"), tall, whole, whole, whole, rows,
    )
    out_specs = (
        rows, rows, cols, cols, cols, tall, whole, whole,
        cols, P("tensor"), tall, whole, whole, whole,
    )
    return jax.shard_map(
        functools.partial(shards, mesh.shape["dp"]), mesh=mesh, in_specs=in_specs, out_specs=out_specs,
        check_vma=False,
    )
```
